32 devices in a mesh: dp: 4 (over x, core), tensor: 4 (over z), pipe: 2 (over y).
Axes of the slice: x: 2, y: 2, z: 4, core: 2. Of those that a mesh axis runs over, the one named last changes fastest.
Arguments:
- attn_policy: bfloat16 [4, 256, 4608], P('dp', 'pipe', 'tensor'), may hold values from -0.046875 to 0.046875
- attn_frozen: bfloat16 [4, 256, 4608], P('dp', 'pipe', 'tensor'), may hold values from -0.046875 to 0.046875
- readout: bfloat16 [4, 256, 8192], P('dp', 'pipe'), may hold values from -6 to 6
- rest_policy: float32 [4, 256], P('dp', 'pipe'), may hold values from -3 to 3
- rest_frozen: float32 [4, 256], P('dp', 'pipe'), may hold values from -3 to 3
- policy_out: bfloat16 [4608, 8192], P('tensor'), may hold values from -0.0625 to 0.0625
- frozen_out: bfloat16 [4608, 8192], P(('tensor', 'dp', 'pipe')), may hold values from -0.0625 to 0.0625
- rewards: float32 [4], replicated, may hold values from -4 to 4
- group_ids: int32 [4], replicated, may hold values from 0 to 1
- prompt_len: int32 [4], replicated, may hold values from 1 to 63
- response_len: int32 [4], replicated, may hold values from 64 to 192
Outputs:
- upstream_grad: bfloat16 [4, 256, 4608], P('dp', 'pipe', 'tensor')
The draws below stay inside these ranges and needn't reach their ends.
Inputs may be any that keep to these rules, and one draw needn't show every extreme that they name: `prompt_len`: prompt and response together fit in a rollout.
All inputs are finite; a program needn't handle non-finite values.
Results may differ from the reference program's by a relative error of at most 0.001.
Values may be sent and summed in bfloat16 or wider, within the bound.
A program may use at most 128 MiB of HBM per device.

```python
import jax
import jax.numpy as jnp
from jax import lax

D = 8192
TOK_DEV = 128
QDIM = 4608
SEQ = 256
NSEQ = 4
GROUPS = 2


def with_ends(entries, rng, low, largest):
    index_at = [jax.random.randint(jax.random.fold_in(rng, axis), (), 0, length) for axis, length in enumerate(entries.shape)]
    longest = entries.shape.index(max(entries.shape))
    next_to = index_at[:longest] + [(index_at[longest] + 1) % entries.shape[longest]] + index_at[longest + 1:]
    return entries.at[tuple(index_at)].set(low).at[tuple(next_to)].set(largest)


def block_levels(rng, extent, cuts, least, top_value):
    def one(axis_at, blocks):
        steps = jax.random.uniform(jax.random.fold_in(jax.random.fold_in(rng, 6), axis_at), (blocks,), jnp.float32, least / len(cuts), top_value / len(cuts))
        return jnp.repeat(jnp.exp(steps), extent[axis_at] // blocks).reshape((-1,) + (1,) * (len(extent) - axis_at - 1))

    loudness = one(*cuts[0])
    for cut in cuts[1:]:
        loudness = loudness * one(*cut)
    return loudness


def scatter_about(key, dims, spread, limit, split=(), kind=jnp.bfloat16):
    level = block_levels(key, dims, split, -0.22, 0.18) if split else 1.0
    values = jax.random.normal(key, dims, jnp.float32) * spread * level
    return jnp.minimum(jnp.maximum(values, -limit), limit).astype(kind)


def setup_inputs(seed: int = 0) -> dict:
    key_of = jax.random.split(jax.random.key(seed), 12)
    attn_policy = scatter_about(key_of[0], (NSEQ, SEQ, QDIM), (QDIM * 4) ** -0.5, 0.046875, ((0, 4), (1, 2), (2, 4)))
    attn_frozen = scatter_about(key_of[1], (NSEQ, SEQ, QDIM), (QDIM * 4) ** -0.5, 0.046875, ((0, 4), (1, 2), (2, 4)))
    readout = scatter_about(key_of[2], (NSEQ, SEQ, D), 1.0, 6.0, ((0, 4), (1, 2)))
    rest_policy = scatter_about(key_of[3], (NSEQ, SEQ), 0.5, 3.0, ((0, 4), (1, 2)), jnp.float32)
    rest_frozen = scatter_about(key_of[4], (NSEQ, SEQ), 0.5, 3.0, ((0, 4), (1, 2)), jnp.float32)
    policy_out = scatter_about(key_of[5], (QDIM, D), D ** -0.5, 0.0625, ((0, 4),))
    frozen_out = scatter_about(key_of[6], (QDIM, D), D ** -0.5, 0.0625, ((0, 32),))
    rewards = scatter_about(key_of[7], (NSEQ,), 1.0, 4.0, (), jnp.float32)
    group_ids = with_ends(jax.random.randint(key_of[8], (NSEQ,), 0, GROUPS), jax.random.fold_in(key_of[8], 1), 0, GROUPS - 1).astype(jnp.int32)
    prompt_len = with_ends(jax.random.randint(key_of[9], (NSEQ,), 1, SEQ // 4), jax.random.fold_in(key_of[9], 1), 1, (SEQ // 4) - 1).astype(jnp.int32)
    response_len = with_ends(jax.random.randint(key_of[10], (NSEQ,), SEQ // 4, 3 * SEQ // 4 + 1), jax.random.fold_in(key_of[10], 1), SEQ // 4, (3 * SEQ // 4 + 1) - 1).astype(jnp.int32)
    return {"attn_policy": attn_policy, "attn_frozen": attn_frozen, "readout": readout, "rest_policy": rest_policy, "rest_frozen": rest_frozen, "policy_out": policy_out, "frozen_out": frozen_out, "rewards": rewards, "group_ids": group_ids, "prompt_len": prompt_len, "response_len": response_len}


KL_WEIGHT = 0.1


def reference(attn_policy, attn_frozen, readout, rest_policy, rest_frozen, policy_out, frozen_out, rewards, group_ids, prompt_len, response_len):
    same_group = (group_ids[:, None] == group_ids[None, :]).astype(jnp.float32)
    group_mean = jnp.dot(same_group, rewards, precision=lax.Precision.HIGHEST) / jnp.sum(same_group, axis=1)
    advantage = rewards - group_mean
    positions = jnp.arange(SEQ, dtype=jnp.int32)

    def per_sequence(items):
        att_policy, att_frozen, unembed, base_policy, base_frozen, adv_one, start_one, length_one = items
        view_policy = jnp.dot(unembed, policy_out.T, preferred_element_type=jnp.float32)
        view_frozen = jnp.dot(unembed, frozen_out.T, preferred_element_type=jnp.float32)
        logp_policy = base_policy + jnp.sum(att_policy.astype(jnp.float32) * view_policy, axis=1)
        logp_frozen = base_frozen + jnp.sum(att_frozen.astype(jnp.float32) * view_frozen, axis=1)
        inside = (positions >= start_one) & (positions < start_one + length_one)
        weighting = jnp.where(inside, SEQ / length_one.astype(jnp.float32), 0.0)
        log_ratio = logp_frozen - logp_policy
        slope = weighting * (KL_WEIGHT * (1.0 - jnp.exp(log_ratio)) - adv_one)
        return (slope[:, None] * view_policy).astype(jnp.bfloat16)

    grads = lax.map(per_sequence, (attn_policy, attn_frozen, readout, rest_policy, rest_frozen, advantage, prompt_len, response_len))
    return jnp.roll(grads, -TOK_DEV, axis=1)
```

```python
import functools

import jax
import jax.numpy as jnp
from jax import lax
from jax.experimental import pallas as pl
from jax.experimental.pallas import tpu as pltpu
from jax.sharding import PartitionSpec as P

KL_WEIGHT = 0.1
MESH = pl.DeviceIdType.MESH

SLOTS = [(e >> 2 & 1, e >> 1 & 1, e & 1) for e in range(8)]


def related(dp, pipe, bits):
    x, y, c = bits
    other_x = lax.rem(dp // 2 + x, 2)
    other_c = lax.rem(lax.rem(dp, 2) + c, 2)
    return other_x * 2 + other_c, lax.rem(pipe + y, 2)


def nt_dot(a, b):
    return lax.dot_general(a, b, (((1,), (1,)), ((), ())), preferred_element_type=jnp.float32)


def as_row(column):
    size = column.shape[0]
    return jnp.transpose(jnp.broadcast_to(column, (size, size)))[:1]


def column_kernel(
    n_t,
    attn_p, attn_f, readout, rest_p, rest_f, policy, frozen,
    rewards, groups, prompts, responses,
    out,
    abuf, rbuf, fbuf, pbuf, own, attn, view, rest, psend, precv, zsend, zrecv, grad,
    fs, fr, as_, ar, hs, hr, rs, rr, zs, zr, ps, pr, qs, qr, gs, gr, ls, lp,
):
    dp, pipe, ten = lax.axis_index("dp"), lax.axis_index("pipe"), lax.axis_index("tensor")
    n_pipe = 2
    me = dp * n_pipe + pipe
    core = lax.rem(dp, 2)
    tokens = readout.shape[1]
    rows = frozen.shape[0]
    wide = rbuf.shape[2]
    part = wide // n_t
    half = tokens // 2
    peers = [related(dp, pipe, bits) for bits in SLOTS]
    index = [p[0] * n_pipe + p[1] for p in peers]
    place = [{"dp": p[0], "pipe": p[1]} for p in peers]
    column = [{"tensor": lax.rem(ten + j, n_t)} for j in range(n_t)]

    def remote(source, target, send, receive, where):
        return pltpu.make_async_remote_copy(
            src_ref=source, dst_ref=target, send_sem=send, recv_sem=receive,
            device_id=where, device_id_type=MESH,
        )

    def cols(start, size):
        return pl.ds(pl.multiple_of(start, 128), size)

    barrier = pltpu.get_barrier_semaphore()
    for where in place[1:] + column[1:]:
        pl.semaphore_signal(barrier, inc=1, device_id=where, device_id_type=MESH)

    locals_ = [
        pltpu.make_async_copy(readout.at[0], own, ls.at[0]),
        pltpu.make_async_copy(attn_p.at[0], attn, ls.at[1]),
        pltpu.make_async_copy(rest_p, rest.at[0], ls.at[2]),
        pltpu.make_async_copy(rest_f, rest.at[1], ls.at[3]),
        pltpu.make_async_copy(readout.at[0, :, cols(me * wide, wide)], rbuf.at[0], ls.at[4]),
        pltpu.make_async_copy(attn_f.at[0], abuf.at[0], ls.at[5]),
        pltpu.make_async_copy(
            frozen.at[:, cols(me * wide, wide)], fbuf.at[pl.ds(pl.multiple_of(me * rows, 16), rows)], ls.at[6]
        ),
    ]
    for copy in locals_:
        copy.start()
    chunks = policy.shape[1] // wide
    loads = [
        pltpu.make_async_copy(policy.at[:, pl.ds(j * wide, wide)], pbuf.at[j], lp.at[j])
        for j in range(chunks)
    ]
    for copy in loads:
        copy.start()

    pl.semaphore_wait(barrier, len(place) - 1 + n_t - 1)

    mine = cols(ten * part, part)
    r_copies = {}
    for s in (6, 7, 4, 5, 2, 3):
        r_copies[s] = remote(
            readout.at[0, :, cols(index[s] * wide + ten * part, part)],
            rbuf.at[s, :, mine], rs.at[s], rr.at[s], place[s],
        )
    r_copies[1] = remote(
        readout.at[0, :, cols(index[1] * wide, wide)], rbuf.at[1], rs.at[1], rr.at[1], place[1]
    )
    a_copies, f_copies = {}, {}
    for s in (6, 7, 4, 5, 2, 3):
        other_core = lax.rem(core + SLOTS[s][2], 2)
        block = pl.ds(pl.multiple_of(other_core * half, half), half)
        a_copies[s] = remote(
            attn_f.at[0, block], abuf.at[s, block], as_.at[s], ar.at[s], place[s]
        )
    a_copies[1] = remote(attn_f.at[0], abuf.at[1], as_.at[1], ar.at[1], place[1])
    for s in (6, 7, 4, 5, 2, 3, 1):
        f_copies[s] = remote(
            frozen.at[:, cols(index[s] * wide, wide)],
            fbuf.at[pl.ds(pl.multiple_of(me * rows, 16), rows)],
            fs.at[s], fr.at[s], place[s],
        )
    for s in (6, 7, 4, 5, 2, 3):
        r_copies[s].start()
    for s in (6, 7, 4, 5, 2, 3):
        a_copies[s].start()
    for s in (6, 7, 4, 5, 2, 3):
        f_copies[s].start()
    for s in (1,):
        r_copies[s].start()
        a_copies[s].start()
        f_copies[s].start()

    for s in (2, 3, 4, 5, 6, 7):
        r_copies[s].wait_recv()
    z_copies = [
        remote(
            rbuf.at[pl.ds(2, 6), :, mine], rbuf.at[pl.ds(2, 6), :, mine], zs.at[j], zr.at[j], column[j]
        )
        for j in range(1, n_t)
    ]
    for copy in z_copies:
        copy.start()
    block = pl.ds(pl.multiple_of(core * half, half), half)
    h_copies = []
    for s in (2, 3, 4, 5, 6, 7):
        a_copies[s].wait_recv()
        h_copies.append(
            remote(abuf.at[s, block], abuf.at[s ^ 1, block], hs.at[s], hr.at[s ^ 1], place[1])
        )
        h_copies[-1].start()

    for copy in locals_:
        copy.wait()
    view[...] = jnp.zeros_like(view)

    def policy_step(j, carry):
        pltpu.make_async_copy(policy.at[:, cols(j * wide, wide)], pbuf.at[j], lp.at[j]).wait()
        view[...] += nt_dot(own[:, cols(j * wide, wide)], pbuf[j])
        return carry

    lax.fori_loop(0, chunks, policy_step, 0)
    part_policy = jnp.sum(attn[...].astype(jnp.float32) * view[...], axis=1, keepdims=True)

    for s in (1, 2, 3, 4, 5, 6, 7):
        f_copies[s].wait_recv()
    a_copies[1].wait_recv()
    r_copies[1].wait_recv()
    for copy in h_copies:
        copy.wait_recv()
    for copy in z_copies:
        copy.wait_recv()

    def frozen_step(s, carry):
        partial = jnp.dot(abuf[s], fbuf[...], preferred_element_type=jnp.float32)
        total = jnp.sum(partial * rbuf[s].astype(jnp.float32), axis=1, keepdims=True)
        psend[s] = jnp.broadcast_to(as_row(total), psend.shape[1:])
        return carry

    lax.fori_loop(0, 8, frozen_step, 0)
    p_copies = [
        remote(psend.at[s], precv.at[s], ps.at[s], pr.at[s], place[s]) for s in range(1, 8)
    ]
    for copy in p_copies:
        copy.start()
    row_policy = jnp.broadcast_to(as_row(part_policy), psend.shape[1:])
    total = psend[0]
    for copy, s in zip(p_copies, range(1, 8)):
        copy.wait_recv()
        total += precv[s]
    which = lax.broadcasted_iota(jnp.int32, total.shape, 0)
    zsend[...] = jnp.where(which == 0, row_policy, total)
    q_copies = [
        remote(zsend, zrecv.at[j], qs.at[j], qr.at[j], column[j]) for j in range(1, n_t)
    ]
    for copy in q_copies:
        copy.start()

    mine_group = groups[dp]
    sum_group, in_group = jnp.float32(0), jnp.float32(0)
    for i in range(rewards.shape[0]):
        same = jnp.where(groups[i] == mine_group, jnp.float32(1), jnp.float32(0))
        sum_group += same * rewards[i]
        in_group += same
    def spread(value):
        return jnp.full((1, tokens), value)
    adv = spread(rewards[dp]) - spread(sum_group) / spread(in_group)
    start, length = prompts[dp], responses[dp]
    position = pipe * tokens + lax.broadcasted_iota(jnp.int32, (1, tokens), 1)
    inside = (position >= start) & (position < start + length)
    seq_total = tokens * n_pipe
    weighting = jnp.where(
        inside, jnp.float32(seq_total) / spread(length.astype(jnp.float32)), jnp.float32(0)
    )

    both = zsend[...]
    for copy, j in zip(q_copies, range(1, n_t)):
        copy.wait_recv()
        both += zrecv[j]
    log_ratio = (rest[1] + both[1:2]) - (rest[0] + both[0:1])
    slope = weighting * (KL_WEIGHT * (1.0 - jnp.exp(log_ratio)) - adv)
    slope = jnp.transpose(jnp.broadcast_to(slope, (tokens, tokens)))
    for j in range(view.shape[1] // tokens):
        at = slice(j * tokens, (j + 1) * tokens)
        grad[:, at] = (slope * view[:, at]).astype(jnp.bfloat16)
    last = remote(grad, out.at[0], gs, gr, place[2])
    last.start()
    for copies in (r_copies.values(), a_copies.values(), f_copies.values(), z_copies, h_copies, p_copies, q_copies):
        for copy in copies:
            copy.wait_send()
    last.wait()


def column_plan(n_t, *args):
    attn_policy, readout, frozen_out = args[0], args[2], args[6]
    tokens, width = readout.shape[1:]
    features = attn_policy.shape[2]
    wide = width // 8
    any_space = pl.BlockSpec(memory_space=pl.ANY)
    smem = pl.BlockSpec(memory_space=pltpu.SMEM)
    bf16, f32 = jnp.bfloat16, jnp.float32
    sems = lambda n: pltpu.SemaphoreType.DMA((n,))
    return pl.pallas_call(
        functools.partial(column_kernel, n_t),
        out_shape=jax.ShapeDtypeStruct((1, tokens, features), bf16),
        in_specs=[any_space] * 7 + [smem] * 4,
        out_specs=any_space,
        scratch_shapes=[
            pltpu.VMEM((8, tokens, features), bf16),
            pltpu.VMEM((8, tokens, wide), bf16),
            pltpu.VMEM((features, wide), bf16),
            pltpu.VMEM((8, features, wide), bf16),
            pltpu.VMEM((tokens, width), bf16),
            pltpu.VMEM((tokens, features), bf16),
            pltpu.VMEM((tokens, features), f32),
            pltpu.VMEM((2, 1, tokens), f32),
            pltpu.VMEM((8, 8, tokens), f32),
            pltpu.VMEM((8, 8, tokens), f32),
            pltpu.VMEM((8, tokens), f32),
            pltpu.VMEM((n_t, 8, tokens), f32),
            pltpu.VMEM((tokens, features), bf16),
        ]
        + [sems(8)] * 8
        + [sems(n_t)] * 2
        + [sems(8)] * 2
        + [sems(n_t)] * 2
        + [pltpu.SemaphoreType.DMA] * 2
        + [sems(7), sems(8)],
        compiler_params=pltpu.CompilerParams(
            collective_id=0, has_side_effects=True, vmem_limit_bytes=52 * 2**20
        ),
        cost_estimate=pl.CostEstimate(
            flops=4 * tokens * features * width, bytes_accessed=2 * features * width + 4 * tokens * width,
            transcendentals=tokens,
        ),
    )(*args)


def shifted(array, axis, by):
    size = lax.axis_size(axis)
    return lax.ppermute(array, axis, [(i, (i + by) % size) for i in range(size)])


def gather_plan(
    attn_policy,
    attn_frozen,
    readout,
    rest_policy,
    rest_frozen,
    policy_out,
    frozen_out,
    rewards,
    group_ids,
    prompt_len,
    response_len,
):
    unembed = readout[0]
    local_tokens = unembed.shape[0]
    view_policy = jnp.dot(unembed, policy_out.T, preferred_element_type=jnp.float32)
    part_policy = jnp.sum(attn_policy[0].astype(jnp.float32) * view_policy, axis=1)
    frozen_rows = lax.all_gather(frozen_out, ("dp", "pipe"), axis=0, tiled=True)
    view_frozen = jnp.dot(unembed, frozen_rows.T, preferred_element_type=jnp.float32)
    part_frozen = jnp.sum(attn_frozen[0].astype(jnp.float32) * view_frozen, axis=1)
    part_policy, part_frozen = lax.psum((part_policy, part_frozen), "tensor")
    logp_policy = rest_policy[0] + part_policy
    logp_frozen = rest_frozen[0] + part_frozen
    same_group = (group_ids[:, None] == group_ids[None, :]).astype(jnp.float32)
    group_mean = jnp.dot(same_group, rewards, precision=lax.Precision.HIGHEST) / jnp.sum(
        same_group, axis=1
    )
    advantage = rewards - group_mean
    seq_index = lax.axis_index("dp")
    seq_ids = jnp.arange(rewards.shape[0], dtype=jnp.int32)
    chosen = seq_ids == seq_index
    adv_one = jnp.sum(jnp.where(chosen, advantage, 0.0))
    start_one = jnp.sum(jnp.where(chosen, prompt_len, 0))
    length_one = jnp.sum(jnp.where(chosen, response_len, 0))
    seq_total = local_tokens * lax.axis_size("pipe")
    positions = lax.axis_index("pipe") * local_tokens + jnp.arange(local_tokens, dtype=jnp.int32)
    inside = (positions >= start_one) & (positions < start_one + length_one)
    weighting = jnp.where(inside, seq_total / length_one.astype(jnp.float32), 0.0)
    log_ratio = logp_frozen - logp_policy
    slope = weighting * (KL_WEIGHT * (1.0 - jnp.exp(log_ratio)) - adv_one)
    token_grad = (slope[:, None] * view_policy).astype(jnp.bfloat16)
    received = shifted(token_grad, "pipe", -1)
    return received[None]


def shards(*args):
    n_dp, n_pipe, n_t = (lax.axis_size(axis) for axis in ("dp", "pipe", "tensor"))
    tokens, width = args[2].shape[1:]
    if (n_dp, n_pipe) == (4, 2) and width % (8 * n_t * 128) == 0 and args[6].shape[0] % 16 == 0 and tokens == 128:
        return column_plan(n_t, *args)
    return gather_plan(*args)


def solution(mesh):
    placed = (
        P("dp", "pipe", "tensor"),
        P("dp", "pipe", "tensor"),
        P("dp", "pipe", None),
        P("dp", "pipe"),
        P("dp", "pipe"),
        P("tensor", None),
        P(("tensor", "dp", "pipe"), None),
        P(),
        P(),
        P(),
        P(),
    )
    return jax.shard_map(
        shards, mesh=mesh, in_specs=placed, out_specs=P("dp", "pipe", "tensor"), check_vma=False
    )
```

```python
import functools

import jax
import jax.numpy as jnp
from jax import lax
from jax.experimental import pallas as pl
from jax.experimental.pallas import tpu as pltpu
from jax.sharding import PartitionSpec as P

KL_WEIGHT = 0.1
MESH = pl.DeviceIdType.MESH

SLOTS = [(e >> 2 & 1, e >> 1 & 1, e & 1) for e in range(8)]


def related(dp, pipe, bits):
    x, y, c = bits
    other_x = lax.rem(dp // 2 + x, 2)
    other_c = lax.rem(lax.rem(dp, 2) + c, 2)
    return other_x * 2 + other_c, lax.rem(pipe + y, 2)


def nt_dot(a, b):
    return lax.dot_general(a, b, (((1,), (1,)), ((), ())), preferred_element_type=jnp.float32)


def as_row(column):
    size = column.shape[0]
    return jnp.transpose(jnp.broadcast_to(column, (size, size)))[:1]


def column_kernel(
    n_t,
    attn_p, attn_f, readout, rest_p, rest_f, policy, frozen,
    rewards, groups, prompts, responses,
    out,
    abuf, rbuf, fbuf, pbuf, own, attn, view, rest, psend, precv, zsend, zrecv, grad,
    fs, fr, as_, ar, hs, hr, rs, rr, zs, zr, ps, pr, qs, qr, gs, gr, ls, lp,
):
    dp, pipe, ten = lax.axis_index("dp"), lax.axis_index("pipe"), lax.axis_index("tensor")
    n_pipe = 2
    me = dp * n_pipe + pipe
    core = lax.rem(dp, 2)
    tokens = readout.shape[1]
    rows = frozen.shape[0]
    wide = rbuf.shape[2]
    part = wide // n_t
    half = tokens // 2
    peers = [related(dp, pipe, bits) for bits in SLOTS]
    index = [p[0] * n_pipe + p[1] for p in peers]
    place = [{"dp": p[0], "pipe": p[1]} for p in peers]
    column = [{"tensor": lax.rem(ten + j, n_t)} for j in range(n_t)]
    everyone = {(s, j): {**place[s], **column[j]} for s in range(8) for j in range(n_t)}

    def remote(source, target, send, receive, where):
        return pltpu.make_async_remote_copy(
            src_ref=source, dst_ref=target, send_sem=send, recv_sem=receive,
            device_id=where, device_id_type=MESH,
        )

    def cols(start, size):
        return pl.ds(pl.multiple_of(start, 128), size)

    barrier = pltpu.get_barrier_semaphore()
    for where in list(everyone.values())[1:]:
        pl.semaphore_signal(barrier, inc=1, device_id=where, device_id_type=MESH)

    locals_ = [
        pltpu.make_async_copy(readout.at[0], own, ls.at[0]),
        pltpu.make_async_copy(attn_p.at[0], attn, ls.at[1]),
        pltpu.make_async_copy(rest_p, rest.at[0], ls.at[2]),
        pltpu.make_async_copy(rest_f, rest.at[1], ls.at[3]),
        pltpu.make_async_copy(readout.at[0, :, cols(me * wide, wide)], rbuf.at[0], ls.at[4]),
        pltpu.make_async_copy(attn_f.at[0], abuf.at[0], ls.at[5]),
        pltpu.make_async_copy(
            frozen.at[:, cols(me * wide, wide)], fbuf.at[pl.ds(pl.multiple_of(me * rows, 16), rows)], ls.at[6]
        ),
    ]
    for copy in locals_:
        copy.start()
    chunks = policy.shape[1] // wide
    loads = [
        pltpu.make_async_copy(policy.at[:, pl.ds(j * wide, wide)], pbuf.at[j], lp.at[j])
        for j in range(chunks)
    ]
    for copy in loads:
        copy.start()

    pl.semaphore_wait(barrier, 8 * n_t - 1)

    mine = cols(ten * part, part)
    r_copies = {}
    for s in (6, 7, 4, 5, 2, 3):
        r_copies[s] = remote(
            readout.at[0, :, cols(index[s] * wide + ten * part, part)],
            rbuf.at[s, :, mine], rs.at[s], rr.at[s], place[s],
        )
    r_copies[1] = remote(
        readout.at[0, :, cols(index[1] * wide, wide)], rbuf.at[1], rs.at[1], rr.at[1], place[1]
    )
    a_copies, f_copies = {}, {}
    for s in (6, 7, 4, 5, 2, 3):
        other_core = lax.rem(core + SLOTS[s][2], 2)
        block = pl.ds(pl.multiple_of(other_core * half, half), half)
        a_copies[s] = remote(
            attn_f.at[0, block], abuf.at[s, block], as_.at[s], ar.at[s], place[s]
        )
    a_copies[1] = remote(attn_f.at[0], abuf.at[1], as_.at[1], ar.at[1], place[1])
    for s in (6, 7, 4, 5, 2, 3, 1):
        f_copies[s] = remote(
            frozen.at[:, cols(index[s] * wide, wide)],
            fbuf.at[pl.ds(pl.multiple_of(me * rows, 16), rows)],
            fs.at[s], fr.at[s], place[s],
        )
    for s in (6, 7, 4, 5, 2, 3):
        r_copies[s].start()
    for s in (6, 7, 4, 5, 2, 3):
        f_copies[s].start()
    for s in (6, 7, 4, 5, 2, 3):
        a_copies[s].start()
    r_copies[1].start()
    a_copies[1].start()
    f_copies[1].start()

    chips = (6, 4, 2)
    z_copies = {}
    for s in chips:
        r_copies[s].wait_recv()
        r_copies[s + 1].wait_recv()
        for j in range(1, n_t):
            block = rbuf.at[pl.ds(s, 2), :, mine]
            z_copies[s, j] = remote(block, block, zs.at[(s // 2 - 1) * n_t + j], zr.at[(s // 2 - 1) * n_t + j], column[j])
            z_copies[s, j].start()

    for copy in locals_:
        copy.wait()
    view[...] = jnp.zeros_like(view)

    def policy_step(j, carry):
        pltpu.make_async_copy(policy.at[:, cols(j * wide, wide)], pbuf.at[j], lp.at[j]).wait()
        view[...] += nt_dot(own[:, cols(j * wide, wide)], pbuf[j])
        return carry

    lax.fori_loop(0, chunks, policy_step, 0)
    part_policy = jnp.sum(attn[...].astype(jnp.float32) * view[...], axis=1, keepdims=True)

    zsend[...] = as_row(part_policy)
    q_copies = [
        remote(zsend, zrecv.at[j], qs.at[j], qr.at[j], column[j]) for j in range(1, n_t)
    ]
    for copy in q_copies:
        copy.start()

    p_copies = []

    def frozen_step(s):
        partial = jnp.dot(abuf[s], fbuf[...], preferred_element_type=jnp.float32)
        total = jnp.sum(partial * rbuf[s].astype(jnp.float32), axis=1, keepdims=True)
        psend[s] = as_row(total)
        for j in range(n_t):
            if s or j:
                p_copies.append(
                    remote(
                        psend.at[s], precv.at[s, j], ps.at[s * n_t + j], pr.at[s * n_t + j], everyone[s, j]
                    )
                )
                p_copies[-1].start()

    half_block = pl.ds(pl.multiple_of(core * half, half), half)
    h_copies = {}

    def pass_on(chip):
        for s in (chip, chip + 1):
            a_copies[s].wait_recv()
            h_copies[s] = remote(
                abuf.at[s, half_block], abuf.at[s ^ 1, half_block], hs.at[s], hr.at[s ^ 1], place[1]
            )
            h_copies[s].start()

    def remote_chip(chip):
        for j in range(1, n_t):
            z_copies[chip, j].wait_recv()
        for s in (chip, chip + 1):
            h_copies[s ^ 1].wait_recv()
        for s in (chip, chip + 1):
            frozen_step(s)

    for s in (1, 2, 3, 4, 5, 6, 7):
        f_copies[s].wait_recv()
    frozen_step(0)
    a_copies[1].wait_recv()
    r_copies[1].wait_recv()
    frozen_step(1)
    pass_on(chips[0])
    pass_on(chips[1])
    remote_chip(chips[0])
    pass_on(chips[2])
    remote_chip(chips[1])
    remote_chip(chips[2])

    mine_group = groups[dp]
    sum_group, in_group = jnp.float32(0), jnp.float32(0)
    for i in range(rewards.shape[0]):
        same = jnp.where(groups[i] == mine_group, jnp.float32(1), jnp.float32(0))
        sum_group += same * rewards[i]
        in_group += same
    def spread(value):
        return jnp.full((1, tokens), value)
    adv = spread(rewards[dp]) - spread(sum_group) / spread(in_group)
    start, length = prompts[dp], responses[dp]
    position = pipe * tokens + lax.broadcasted_iota(jnp.int32, (1, tokens), 1)
    inside = (position >= start) & (position < start + length)
    seq_total = tokens * n_pipe
    weighting = jnp.where(
        inside, jnp.float32(seq_total) / spread(length.astype(jnp.float32)), jnp.float32(0)
    )

    policy_sum = zsend[...]
    for copy, j in zip(q_copies, range(1, n_t)):
        copy.wait_recv()
        policy_sum += zrecv[j]
    for copy in p_copies:
        copy.wait_recv()
    frozen_sum = psend[0]
    for s in range(8):
        for j in range(n_t):
            if s or j:
                frozen_sum += precv[s, j]
    log_ratio = (rest[1] + frozen_sum) - (rest[0] + policy_sum)
    slope = weighting * (KL_WEIGHT * (1.0 - jnp.exp(log_ratio)) - adv)
    slope = jnp.transpose(jnp.broadcast_to(slope, (tokens, tokens)))
    for j in range(view.shape[1] // tokens):
        at = slice(j * tokens, (j + 1) * tokens)
        grad[:, at] = (slope * view[:, at]).astype(jnp.bfloat16)
    last = remote(grad, out.at[0], gs, gr, place[2])
    last.start()
    for copies in (r_copies.values(), a_copies.values(), f_copies.values(), z_copies.values(), h_copies.values(), p_copies, q_copies):
        for copy in copies:
            copy.wait_send()
    last.wait()


def column_plan(n_t, *args):
    attn_policy, readout, frozen_out = args[0], args[2], args[6]
    tokens, width = readout.shape[1:]
    features = attn_policy.shape[2]
    wide = width // 8
    any_space = pl.BlockSpec(memory_space=pl.ANY)
    smem = pl.BlockSpec(memory_space=pltpu.SMEM)
    bf16, f32 = jnp.bfloat16, jnp.float32
    sems = lambda n: pltpu.SemaphoreType.DMA((n,))
    return pl.pallas_call(
        functools.partial(column_kernel, n_t),
        out_shape=jax.ShapeDtypeStruct((1, tokens, features), bf16),
        in_specs=[any_space] * 7 + [smem] * 4,
        out_specs=any_space,
        scratch_shapes=[
            pltpu.VMEM((8, tokens, features), bf16),
            pltpu.VMEM((8, tokens, wide), bf16),
            pltpu.VMEM((features, wide), bf16),
            pltpu.VMEM((8, features, wide), bf16),
            pltpu.VMEM((tokens, width), bf16),
            pltpu.VMEM((tokens, features), bf16),
            pltpu.VMEM((tokens, features), f32),
            pltpu.VMEM((2, 1, tokens), f32),
            pltpu.VMEM((8, 1, tokens), f32),
            pltpu.VMEM((8, n_t, 1, tokens), f32),
            pltpu.VMEM((1, tokens), f32),
            pltpu.VMEM((n_t, 1, tokens), f32),
            pltpu.VMEM((tokens, features), bf16),
        ]
        + [sems(8)] * 8
        + [sems(3 * n_t)] * 2
        + [sems(8 * n_t)] * 2
        + [sems(n_t)] * 2
        + [pltpu.SemaphoreType.DMA] * 2
        + [sems(7), sems(8)],
        compiler_params=pltpu.CompilerParams(
            collective_id=0, has_side_effects=True, vmem_limit_bytes=60 * 2**20
        ),
        cost_estimate=pl.CostEstimate(
            flops=4 * tokens * features * width, bytes_accessed=2 * features * width + 4 * tokens * width,
            transcendentals=tokens,
        ),
    )(*args)


def shifted(array, axis, by):
    size = lax.axis_size(axis)
    return lax.ppermute(array, axis, [(i, (i + by) % size) for i in range(size)])


def gather_plan(
    attn_policy,
    attn_frozen,
    readout,
    rest_policy,
    rest_frozen,
    policy_out,
    frozen_out,
    rewards,
    group_ids,
    prompt_len,
    response_len,
):
    unembed = readout[0]
    local_tokens = unembed.shape[0]
    view_policy = jnp.dot(unembed, policy_out.T, preferred_element_type=jnp.float32)
    part_policy = jnp.sum(attn_policy[0].astype(jnp.float32) * view_policy, axis=1)
    frozen_rows = lax.all_gather(frozen_out, ("dp", "pipe"), axis=0, tiled=True)
    view_frozen = jnp.dot(unembed, frozen_rows.T, preferred_element_type=jnp.float32)
    part_frozen = jnp.sum(attn_frozen[0].astype(jnp.float32) * view_frozen, axis=1)
    part_policy, part_frozen = lax.psum((part_policy, part_frozen), "tensor")
    logp_policy = rest_policy[0] + part_policy
    logp_frozen = rest_frozen[0] + part_frozen
    same_group = (group_ids[:, None] == group_ids[None, :]).astype(jnp.float32)
    group_mean = jnp.dot(same_group, rewards, precision=lax.Precision.HIGHEST) / jnp.sum(
        same_group, axis=1
    )
    advantage = rewards - group_mean
    seq_index = lax.axis_index("dp")
    seq_ids = jnp.arange(rewards.shape[0], dtype=jnp.int32)
    chosen = seq_ids == seq_index
    adv_one = jnp.sum(jnp.where(chosen, advantage, 0.0))
    start_one = jnp.sum(jnp.where(chosen, prompt_len, 0))
    length_one = jnp.sum(jnp.where(chosen, response_len, 0))
    seq_total = local_tokens * lax.axis_size("pipe")
    positions = lax.axis_index("pipe") * local_tokens + jnp.arange(local_tokens, dtype=jnp.int32)
    inside = (positions >= start_one) & (positions < start_one + length_one)
    weighting = jnp.where(inside, seq_total / length_one.astype(jnp.float32), 0.0)
    log_ratio = logp_frozen - logp_policy
    slope = weighting * (KL_WEIGHT * (1.0 - jnp.exp(log_ratio)) - adv_one)
    token_grad = (slope[:, None] * view_policy).astype(jnp.bfloat16)
    received = shifted(token_grad, "pipe", -1)
    return received[None]


def shards(*args):
    n_dp, n_pipe, n_t = (lax.axis_size(axis) for axis in ("dp", "pipe", "tensor"))
    tokens, width = args[2].shape[1:]
    if (n_dp, n_pipe) == (4, 2) and width % (8 * n_t * 128) == 0 and args[6].shape[0] % 16 == 0 and tokens == 128:
        return column_plan(n_t, *args)
    return gather_plan(*args)


def solution(mesh):
    placed = (
        P("dp", "pipe", "tensor"),
        P("dp", "pipe", "tensor"),
        P("dp", "pipe", None),
        P("dp", "pipe"),
        P("dp", "pipe"),
        P("tensor", None),
        P(("tensor", "dp", "pipe"), None),
        P(),
        P(),
        P(),
        P(),
    )
    return jax.shard_map(
        shards, mesh=mesh, in_specs=placed, out_specs=P("dp", "pipe", "tensor"), check_vma=False
    )
```

```python
import functools

import jax
import jax.numpy as jnp
from jax import lax
from jax.experimental import pallas as pl
from jax.experimental.pallas import tpu as pltpu
from jax.sharding import PartitionSpec as P

KL_WEIGHT = 0.1
EARLY = 2
MESH = pl.DeviceIdType.MESH

SLOTS = [(e >> 2 & 1, e >> 1 & 1, e & 1) for e in range(8)]


def related(dp, pipe, bits):
    x, y, c = bits
    other_x = lax.rem(dp // 2 + x, 2)
    other_c = lax.rem(lax.rem(dp, 2) + c, 2)
    return other_x * 2 + other_c, lax.rem(pipe + y, 2)


def nt_dot(a, b):
    return lax.dot_general(a, b, (((1,), (1,)), ((), ())), preferred_element_type=jnp.float32)


def as_row(column):
    size = column.shape[0]
    return jnp.transpose(jnp.broadcast_to(column, (size, size)))[:1]


def column_kernel(
    n_t,
    attn_p, attn_f, readout, rest_p, rest_f, policy, frozen,
    rewards, groups, prompts, responses,
    out,
    abuf, rbuf, fbuf, pbuf, own, attn, view, rest, psend, precv, zsend, zrecv, grad, vrecv, srow, sgot,
    fs, fr, as_, ar, hs, hr, rs, rr, zs, zr, ps, pr, qs, qr, gs, gr, ls, lp, ws, wr, vs, vr, ss, sr, os,
):
    dp, pipe, ten = lax.axis_index("dp"), lax.axis_index("pipe"), lax.axis_index("tensor")
    n_pipe = 2
    me = dp * n_pipe + pipe
    core = lax.rem(dp, 2)
    tokens = readout.shape[1]
    rows = frozen.shape[0]
    wide = rbuf.shape[2]
    part = wide // n_t
    half = tokens // 2
    features = policy.shape[0]
    cut = features - vrecv.shape[1]
    peers = [related(dp, pipe, bits) for bits in SLOTS]
    index = [p[0] * n_pipe + p[1] for p in peers]
    place = [{"dp": p[0], "pipe": p[1]} for p in peers]
    column = [{"tensor": lax.rem(ten + j, n_t)} for j in range(n_t)]
    everyone = {(s, j): {**place[s], **column[j]} for s in range(8) for j in range(n_t)}

    def remote(source, target, send, receive, where):
        return pltpu.make_async_remote_copy(
            src_ref=source, dst_ref=target, send_sem=send, recv_sem=receive,
            device_id=where, device_id_type=MESH,
        )

    def cols(start, size):
        return pl.ds(pl.multiple_of(start, 128), size)

    barrier = pltpu.get_barrier_semaphore()
    for where in list(everyone.values())[1:]:
        pl.semaphore_signal(barrier, inc=1, device_id=where, device_id_type=MESH)

    locals_ = [
        pltpu.make_async_copy(readout.at[0], own, ls.at[0]),
        pltpu.make_async_copy(attn_p.at[0], attn, ls.at[1]),
        pltpu.make_async_copy(rest_p, rest.at[0], ls.at[2]),
        pltpu.make_async_copy(rest_f, rest.at[1], ls.at[3]),
        pltpu.make_async_copy(readout.at[0, :, cols(me * wide, wide)], rbuf.at[0], ls.at[4]),
        pltpu.make_async_copy(attn_f.at[0], abuf.at[0], ls.at[5]),
        pltpu.make_async_copy(
            frozen.at[:, cols(me * wide, wide)], fbuf.at[pl.ds(pl.multiple_of(me * rows, 16), rows)], ls.at[6]
        ),
    ]
    for copy in locals_:
        copy.start()
    chunks = policy.shape[1] // wide
    loads = [
        pltpu.make_async_copy(policy.at[:, pl.ds(j * wide, wide)], pbuf.at[j], lp.at[j])
        for j in range(chunks)
    ]
    for copy in loads:
        copy.start()

    pl.semaphore_wait(barrier, 8 * n_t - 1)

    mine = cols(ten * part, part)
    r_copies = {}
    for s in (6, 7, 4, 5, 2, 3):
        r_copies[s] = remote(
            readout.at[0, :, cols(index[s] * wide + ten * part, part)],
            rbuf.at[s, :, mine], rs.at[s], rr.at[s], place[s],
        )
    r_copies[1] = remote(
        readout.at[0, :, cols(index[1] * wide, wide)], rbuf.at[1], rs.at[1], rr.at[1], place[1]
    )
    a_copies, f_copies = {}, {}

    def half_of(which):
        return pl.ds(pl.multiple_of(which * half, half), half)

    for turn, along in enumerate((1 - core, core)):
        for e in range(2):
            to_core = lax.rem(core + e, 2)
            to = {
                "dp": lax.rem(dp // 2 + along, 2) * 2 + to_core,
                "pipe": lax.rem(pipe + 1 - along, 2),
            }
            slot = 2 + 2 * along + e
            a_copies[turn, e] = remote(
                attn_f.at[0, half_of(to_core)], abuf.at[slot, half_of(to_core)],
                as_.at[slot], ar.at[slot], to,
            )
    a_copies[1] = remote(attn_f.at[0], abuf.at[1], as_.at[1], ar.at[1], place[1])
    for s in (6, 7, 4, 5, 2, 3, 1):
        f_copies[s] = remote(
            frozen.at[:, cols(index[s] * wide, wide)],
            fbuf.at[pl.ds(pl.multiple_of(me * rows, 16), rows)],
            fs.at[s], fr.at[s], place[s],
        )
    for s in (6, 7, 4, 5, 2, 3):
        r_copies[s].start()
    for e in range(2):
        a_copies[0, e].start()
    for s in (6, 7, 4, 5, 2, 3):
        f_copies[s].start()
    for e in range(2):
        a_copies[1, e].start()
    r_copies[1].start()
    a_copies[1].start()
    f_copies[1].start()

    chips = (6, 4, 2)
    z_copies = {}
    for s in chips:
        r_copies[s].wait_recv()
        r_copies[s + 1].wait_recv()
        for j in range(1, n_t):
            block = rbuf.at[pl.ds(s, 2), :, mine]
            z_copies[s, j] = remote(block, block, zs.at[(s // 2 - 1) * n_t + j], zr.at[(s // 2 - 1) * n_t + j], column[j])
            z_copies[s, j].start()

    half_block = half_of(core)
    h_copies, w_copies = {}, {}

    def arrived(slot):
        block = abuf.at[slot, half_block]
        remote(block, block, as_.at[slot], ar.at[slot], place[1]).wait_recv()

    def pass_on(name, slot, to_slot):
        h_copies[name] = remote(
            abuf.at[slot, half_block], abuf.at[to_slot, half_block], hs.at[slot], hr.at[to_slot], place[1]
        )
        h_copies[name].start()

    def second_hop(name, slot, to_slot, where):
        arrived(slot)
        w_copies[name] = remote(
            abuf.at[slot, half_block], abuf.at[to_slot, half_block], ws.at[name], wr.at[name], where
        )
        w_copies[name].start()

    def from_core(slot):
        block = abuf.at[slot, half_of(1 - core)]
        remote(block, block, hs.at[slot], hr.at[slot], place[1]).wait_recv()

    second_hop(0, 4 + core, 6 + core, place[2])
    second_hop(1, 3 - core, 7 - core, place[4])
    pass_on(0, 4 + core, 5 - core)
    pass_on(1, 3 - core, 2 + core)

    for copy in locals_:
        copy.wait()
    view[...] = jnp.zeros_like(view)

    def policy_step(j, carry):
        pltpu.make_async_copy(policy.at[:, cols(j * wide, wide)], pbuf.at[j], lp.at[j]).wait()
        view[...] += nt_dot(own[:, cols(j * wide, wide)], pbuf[j])
        return carry

    lax.fori_loop(0, chunks, policy_step, 0)
    part_policy = jnp.sum(attn[...].astype(jnp.float32) * view[...], axis=1, keepdims=True)

    zsend[...] = as_row(part_policy)
    q_copies = [
        remote(zsend, zrecv.at[j], qs.at[j], qr.at[j], column[j]) for j in range(1, n_t)
    ]
    for copy in q_copies:
        copy.start()

    p_copies = []

    def frozen_step(s):
        partial = jnp.dot(abuf[s], fbuf[...], preferred_element_type=jnp.float32)
        total = jnp.sum(partial * rbuf[s].astype(jnp.float32), axis=1, keepdims=True)
        psend[s] = as_row(total)
        for j in range(n_t):
            if s or j:
                p_copies.append(
                    remote(
                        psend.at[s], precv.at[s, j], ps.at[s * n_t + j], pr.at[s * n_t + j], everyone[s, j]
                    )
                )
                p_copies[-1].start()

    def remote_chip(chip):
        for j in range(1, n_t):
            z_copies[chip, j].wait_recv()
        for s in (chip, chip + 1):
            from_core(s)
            frozen_step(s)

    for s in (1, 2, 3, 4, 5, 6, 7):
        f_copies[s].wait_recv()
    frozen_step(0)
    a_copies[1].wait_recv()
    r_copies[1].wait_recv()
    frozen_step(1)
    for name in range(2):
        w_copies[name].wait_recv()
    pass_on(2, 6, 7)
    pass_on(3, 7, 6)
    remote_chip(6)
    arrived(5 - core)
    arrived(2 + core)
    pass_on(4, 5 - core, 4 + core)
    pass_on(5, 2 + core, 3 - core)
    early = remote(view.at[:, pl.ds(cut, features - cut)], vrecv, vs, vr, place[2])
    early.start()
    remote_chip(4)
    remote_chip(2)

    mine_group = groups[dp]
    sum_group, in_group = jnp.float32(0), jnp.float32(0)
    for i in range(rewards.shape[0]):
        same = jnp.where(groups[i] == mine_group, jnp.float32(1), jnp.float32(0))
        sum_group += same * rewards[i]
        in_group += same
    def spread(value):
        return jnp.full((1, tokens), value)
    adv = spread(rewards[dp]) - spread(sum_group) / spread(in_group)
    start, length = prompts[dp], responses[dp]
    position = pipe * tokens + lax.broadcasted_iota(jnp.int32, (1, tokens), 1)
    inside = (position >= start) & (position < start + length)
    seq_total = tokens * n_pipe
    weighting = jnp.where(
        inside, jnp.float32(seq_total) / spread(length.astype(jnp.float32)), jnp.float32(0)
    )

    policy_sum = zsend[...]
    for copy, j in zip(q_copies, range(1, n_t)):
        copy.wait_recv()
        policy_sum += zrecv[j]
    for copy in p_copies:
        copy.wait_recv()
    frozen_sum = psend[0]
    for s in range(8):
        for j in range(n_t):
            if s or j:
                frozen_sum += precv[s, j]
    log_ratio = (rest[1] + frozen_sum) - (rest[0] + policy_sum)
    slope = weighting * (KL_WEIGHT * (1.0 - jnp.exp(log_ratio)) - adv)
    srow[...] = slope
    slope_copy = remote(srow, sgot, ss, sr, place[2])
    slope_copy.start()

    def spread_rows(row):
        return jnp.transpose(jnp.broadcast_to(row, (tokens, tokens)))

    slope = spread_rows(slope)
    for j in range(cut // tokens):
        at = slice(j * tokens, (j + 1) * tokens)
        grad[:, at] = (slope * view[:, at]).astype(jnp.bfloat16)
    first = pl.ds(0, cut)
    last = remote(grad.at[:, first], out.at[0, :, first], gs, gr, place[2])
    last.start()
    slope_copy.wait_recv()
    early.wait_recv()
    slope = spread_rows(sgot[...])
    for j in range((features - cut) // tokens):
        at = slice(j * tokens, (j + 1) * tokens)
        grad[:, cut + j * tokens : cut + (j + 1) * tokens] = (slope * vrecv[:, at]).astype(jnp.bfloat16)
    rest_cols = pl.ds(cut, features - cut)
    home = pltpu.make_async_copy(grad.at[:, rest_cols], out.at[0, :, rest_cols], os)
    home.start()
    slope_copy.wait_send()
    early.wait_send()
    for copies in (r_copies.values(), a_copies.values(), f_copies.values(), z_copies.values(), h_copies.values(), w_copies.values(), p_copies, q_copies):
        for copy in copies:
            copy.wait_send()
    last.wait()
    home.wait()


def column_plan(n_t, *args):
    attn_policy, readout, frozen_out = args[0], args[2], args[6]
    tokens, width = readout.shape[1:]
    features = attn_policy.shape[2]
    wide = width // 8
    any_space = pl.BlockSpec(memory_space=pl.ANY)
    smem = pl.BlockSpec(memory_space=pltpu.SMEM)
    bf16, f32 = jnp.bfloat16, jnp.float32
    sems = lambda n: pltpu.SemaphoreType.DMA((n,))
    return pl.pallas_call(
        functools.partial(column_kernel, n_t),
        out_shape=jax.ShapeDtypeStruct((1, tokens, features), bf16),
        in_specs=[any_space] * 7 + [smem] * 4,
        out_specs=any_space,
        scratch_shapes=[
            pltpu.VMEM((8, tokens, features), bf16),
            pltpu.VMEM((8, tokens, wide), bf16),
            pltpu.VMEM((features, wide), bf16),
            pltpu.VMEM((8, features, wide), bf16),
            pltpu.VMEM((tokens, width), bf16),
            pltpu.VMEM((tokens, features), bf16),
            pltpu.VMEM((tokens, features), f32),
            pltpu.VMEM((2, 1, tokens), f32),
            pltpu.VMEM((8, 1, tokens), f32),
            pltpu.VMEM((8, n_t, 1, tokens), f32),
            pltpu.VMEM((1, tokens), f32),
            pltpu.VMEM((n_t, 1, tokens), f32),
            pltpu.VMEM((tokens, features), bf16),
            pltpu.VMEM((tokens, EARLY * tokens), f32),
            pltpu.VMEM((1, tokens), f32),
            pltpu.VMEM((1, tokens), f32),
        ]
        + [sems(8)] * 8
        + [sems(3 * n_t)] * 2
        + [sems(8 * n_t)] * 2
        + [sems(n_t)] * 2
        + [pltpu.SemaphoreType.DMA] * 2
        + [sems(7), sems(8), sems(2), sems(2)]
        + [pltpu.SemaphoreType.DMA] * 5,
        compiler_params=pltpu.CompilerParams(
            collective_id=0, has_side_effects=True, vmem_limit_bytes=60 * 2**20
        ),
        cost_estimate=pl.CostEstimate(
            flops=4 * tokens * features * width, bytes_accessed=2 * features * width + 4 * tokens * width,
            transcendentals=tokens,
        ),
    )(*args)


def shifted(array, axis, by):
    size = lax.axis_size(axis)
    return lax.ppermute(array, axis, [(i, (i + by) % size) for i in range(size)])


def gather_plan(
    attn_policy,
    attn_frozen,
    readout,
    rest_policy,
    rest_frozen,
    policy_out,
    frozen_out,
    rewards,
    group_ids,
    prompt_len,
    response_len,
):
    unembed = readout[0]
    local_tokens = unembed.shape[0]
    view_policy = jnp.dot(unembed, policy_out.T, preferred_element_type=jnp.float32)
    part_policy = jnp.sum(attn_policy[0].astype(jnp.float32) * view_policy, axis=1)
    frozen_rows = lax.all_gather(frozen_out, ("dp", "pipe"), axis=0, tiled=True)
    view_frozen = jnp.dot(unembed, frozen_rows.T, preferred_element_type=jnp.float32)
    part_frozen = jnp.sum(attn_frozen[0].astype(jnp.float32) * view_frozen, axis=1)
    part_policy, part_frozen = lax.psum((part_policy, part_frozen), "tensor")
    logp_policy = rest_policy[0] + part_policy
    logp_frozen = rest_frozen[0] + part_frozen
    same_group = (group_ids[:, None] == group_ids[None, :]).astype(jnp.float32)
    group_mean = jnp.dot(same_group, rewards, precision=lax.Precision.HIGHEST) / jnp.sum(
        same_group, axis=1
    )
    advantage = rewards - group_mean
    seq_index = lax.axis_index("dp")
    seq_ids = jnp.arange(rewards.shape[0], dtype=jnp.int32)
    chosen = seq_ids == seq_index
    adv_one = jnp.sum(jnp.where(chosen, advantage, 0.0))
    start_one = jnp.sum(jnp.where(chosen, prompt_len, 0))
    length_one = jnp.sum(jnp.where(chosen, response_len, 0))
    seq_total = local_tokens * lax.axis_size("pipe")
    positions = lax.axis_index("pipe") * local_tokens + jnp.arange(local_tokens, dtype=jnp.int32)
    inside = (positions >= start_one) & (positions < start_one + length_one)
    weighting = jnp.where(inside, seq_total / length_one.astype(jnp.float32), 0.0)
    log_ratio = logp_frozen - logp_policy
    slope = weighting * (KL_WEIGHT * (1.0 - jnp.exp(log_ratio)) - adv_one)
    token_grad = (slope[:, None] * view_policy).astype(jnp.bfloat16)
    received = shifted(token_grad, "pipe", -1)
    return received[None]


def shards(*args):
    n_dp, n_pipe, n_t = (lax.axis_size(axis) for axis in ("dp", "pipe", "tensor"))
    tokens, width = args[2].shape[1:]
    if (n_dp, n_pipe) == (4, 2) and width % (8 * n_t * 128) == 0 and args[6].shape[0] % 16 == 0 and tokens == 128:
        return column_plan(n_t, *args)
    return gather_plan(*args)


def solution(mesh):
    placed = (
        P("dp", "pipe", "tensor"),
        P("dp", "pipe", "tensor"),
        P("dp", "pipe", None),
        P("dp", "pipe"),
        P("dp", "pipe"),
        P("tensor", None),
        P(("tensor", "dp", "pipe"), None),
        P(),
        P(),
        P(),
        P(),
    )
    return jax.shard_map(
        shards, mesh=mesh, in_specs=placed, out_specs=P("dp", "pipe", "tensor"), check_vma=False
    )
```
